256 devices in a mesh: wide: 32 (over x, z), sib: 8 (over y, core).
Axes of the slice: x: 4, y: 4, z: 8, core: 2. Of those that a mesh axis runs over, the one named last changes fastest.
Arguments:
- points: bfloat16 [1048576, 128], P(('wide', 'sib')), may hold values from -40 to 40
- charges: bfloat16 [1048576, 128], P(('wide', 'sib')), may hold values from -2.5 to 2.5
- skel: int32 [4096, 128], P(('wide', 'sib')), may hold values from 0 to 255, all different within a row
- near_list: int32 [4096, 6], P(('wide', 'sib')), may hold values from 0 to 15, all different within a row
- far_gap: int32 [4096, 4], P(('wide', 'sib')), may hold values from 0 to 30, all different within a row; in each aligned block of 16 rows (0 to 15, 16 to 31, ...) at most 5 rows name the same one
- far_leaf: int32 [4096, 4], P(('wide', 'sib')), may hold values from 0 to 15
- par_pick: int32 [4096, 64], P(('wide', 'sib')), may hold values from 0 to 127, all different within a row
Outputs:
- potential: bfloat16 [1048576, 128], P(('wide', 'sib'))
- transfer: float32 [4096, 128, 128], P(('wide', 'sib'))
The draws below stay inside these ranges and needn't reach their ends.
Inputs may be any that keep to these rules, and one draw needn't show every extreme that they name: `skel`: the 128 numbers of a row are distinct. `near_list`: the 6 numbers of a row are distinct. `far_gap`: the 4 offsets of a row are distinct; over the rows of one device no offset appears more than 5 times, and some offset appears exactly 5 times. `par_pick`: the 64 numbers of a row are distinct.
All inputs are finite; a program needn't handle non-finite values.
Results may differ from the reference program's by a relative error of at most 0.0059.
Values may be sent and summed in bfloat16 or wider, within the bound.
A program may use at most 128 MiB of HBM per device.

```python
import math
import jax
import jax.numpy as jnp
import numpy as np
from jax import lax

DIM = 128
LEAF = 256
R = 128
RHS = 128
LEAVES_DEV = 16
NEAR = 6
FAR = 4
HALF_R = 64
PEERS = 31
CAP = 5
N_LEAVES = 4096
NPTS = 1048576
N_WIDE = 32
N_SIB = 8


def draw_points(key, part):
    key = jax.random.fold_in(key, 11)
    keys = jax.random.split(key, 5)
    order = jax.random.permutation(keys[0], DIM).astype(jnp.float32)
    spread = 0.6 * math.sqrt(DIM) * jnp.exp(-order / 6.0) + 0.3
    pair_count = N_LEAVES // (2 * LEAVES_DEV)
    dev_count = N_LEAVES // LEAVES_DEV
    pair_centre = jnp.clip(jax.random.normal(keys[1], (pair_count, DIM), jnp.float32), -4.0, 4.0)
    dev_centre = jnp.clip(jax.random.normal(keys[2], (dev_count, DIM), jnp.float32), -4.0, 4.0)
    leaf_centre = jnp.clip(jax.random.normal(keys[3], (N_LEAVES, DIM), jnp.float32), -4.0, 4.0)
    centre = 0.42 * jnp.repeat(pair_centre, 2 * LEAVES_DEV, axis=0)
    centre = centre + 0.3 * jnp.repeat(dev_centre, LEAVES_DEV, axis=0) + 0.35 * leaf_centre
    offsets = jnp.clip(jax.random.normal(keys[4], (N_LEAVES, LEAF, DIM), jnp.float32), -4.0, 4.0)
    placed = centre[:, None, :] + spread[None, None, :] * offsets
    return placed.reshape(NPTS, DIM).astype(jnp.bfloat16)


def place_ends(entries, stream_key, smallest, high):
    extent = entries.shape
    place = [jax.random.randint(jax.random.fold_in(stream_key, axis), (), 0, extent[axis]) for axis in range(len(extent))]
    entries = entries.at[tuple(place)].set(smallest)
    longest = extent.index(max(extent))
    place[longest] = (place[longest] + 1) % extent[longest]
    return entries.at[tuple(place)].set(high)


def block_scale(stream_key, dims, pieces, low, largest):
    level, own = 1.0, jax.random.fold_in(stream_key, 6)
    for axis_at, shards_of in pieces:
        heights = jnp.exp(jax.random.uniform(jax.random.fold_in(own, axis_at), (shards_of,), jnp.float32, low / len(pieces), largest / len(pieces)))
        level = level * jnp.repeat(heights, dims[axis_at] // shards_of).reshape([-1 if axis == axis_at else 1 for axis in range(len(dims))])
    return level


def choose_distinct(own_key, rows, amount, top, lift):
    ranking = jax.random.permutation(jax.random.fold_in(own_key, 1), amount)
    pull = ranking
    for power in range(3):
        pull = pull * pull // amount
    pull = pull * lift // amount
    tickets = jax.random.randint(jax.random.fold_in(own_key, 2), (rows, amount), 0, 4096) + pull
    holders = jax.random.permutation(jax.random.fold_in(own_key, 3), rows)[jnp.arange(amount) % rows]
    tickets = jnp.where(jnp.arange(rows)[:, None] == holders[None, :], 1 << 14, tickets)
    merit = tickets * amount + jnp.arange(amount)
    return lax.top_k(merit.astype(jnp.int32), top)[1].astype(jnp.int32)


def deal_out(key, own, number, rows, number_of, top, reach, skew):
    sequence = jax.random.permutation(key, number_of)
    crowded, common = shares(number_of, rows * top, reach, skew, True), shares(number_of, rows * top, reach, skew, False)
    places = jnp.arange(number_of)

    def named(lengths, rotation):
        used = int((lengths > 0).sum())
        fixed = max(1, used // 4)
        passed = fixed + (places - fixed + rotation * (used - fixed)) % max(1, number_of - fixed)
        return jnp.zeros((number_of,), jnp.int32).at[sequence[jnp.where(places < fixed, places, passed)]].set(jnp.asarray(lengths, jnp.int32))

    lengths = jnp.where(number % 4 == 0, named(crowded, number // 4), named(common, number - number // 4 - 1))
    mixed = jax.random.permutation(jax.random.fold_in(own, 3), number_of)
    donor, sink = mixed[0:number_of // 2 * 2:2], mixed[1:number_of // 2 * 2:2]
    margin = jnp.minimum(lengths[donor] - 1, reach - lengths[sink]) // 2
    margin = jnp.where((donor == sequence[0]) | (sink == sequence[0]) | (lengths[sink] == 0), 0, jnp.maximum(margin, 0))
    passed = jax.random.randint(jax.random.fold_in(own, 4), (number_of // 2,), 0, 1 << 20) % (margin + 1)
    lengths = lengths.at[donor].add(-passed).at[sink].add(passed)
    items = jnp.searchsorted(jnp.cumsum(lengths), jnp.arange(rows * top), side="right").astype(jnp.int32)
    table = items.reshape(top, rows).T
    table = table[jax.random.permutation(jax.random.fold_in(own, 1), rows)]
    rotation = jax.random.randint(jax.random.fold_in(own, 2), (rows, 1), 0, top)
    return jnp.take_along_axis(table, (jnp.arange(top)[None, :] + rotation) % top, axis=1)


def shares(number_of, total, limit, skew, full):
    loads = [(1 << 20) // math.isqrt(rank ** skew) + 1 for rank in range(1, number_of + 1)]
    largest = limit if full else min(limit, max(-(-total // number_of), total * loads[0] // sum(loads)))
    least = 1 if total - largest >= number_of - 1 else 0
    holding, rest = [largest] + [least] * (number_of - 1), total - largest - least * (number_of - 1)
    while rest > 0:
        free = [i for i in range(1, number_of) if holding[i] < largest] or [i for i in range(1, number_of) if holding[i] < limit]
        pool, budget = sum([loads[i] for i in free]), rest
        for i in free:
            addition = min(limit - holding[i], max(1, budget * loads[i] // pool), rest)
            holding[i] = holding[i] + addition
            rest = rest - addition
    return np.array(holding)


def centred(own_key, shape, scale, reach, cuts=(), kind=jnp.bfloat16):
    entries = scale * jax.random.normal(own_key, shape, jnp.float32)
    if cuts:
        entries = entries * block_scale(own_key, shape, cuts, -0.22, 0.18)
    return jnp.clip(entries, -reach, reach).astype(kind)


def setup_inputs(seed: int = 0) -> dict:
    seeds = jax.random.split(jax.random.key(seed), 8)
    points = draw_points(jax.random.fold_in(seeds[7], 71), 0)
    charges = centred(seeds[1], (NPTS, RHS), 0.3, 2.5, ((0, 256),))
    skel = choose_distinct(seeds[2], N_LEAVES, LEAF, R, 0)
    near_list = choose_distinct(seeds[3], N_LEAVES, LEAVES_DEV, NEAR, 0)
    far_gap_keys = jax.random.split(jax.random.fold_in(seeds[4], 1), N_LEAVES // LEAVES_DEV)
    far_gap_turns = jax.random.permutation(jax.random.fold_in(seeds[4], 3), N_LEAVES // LEAVES_DEV)
    far_gap = jax.vmap(lambda own, number: deal_out(jax.random.fold_in(seeds[4], 2), own, number, LEAVES_DEV, PEERS, FAR, CAP, 2))(far_gap_keys, far_gap_turns).reshape((N_LEAVES, FAR))
    far_leaf = place_ends(jax.random.randint(seeds[5], (N_LEAVES, FAR), 0, LEAVES_DEV), jax.random.fold_in(seeds[5], 1), 0, LEAVES_DEV - 1).astype(jnp.int32)
    par_pick = choose_distinct(seeds[6], N_LEAVES, R, HALF_R, 0)
    return {"points": points, "charges": charges, "skel": skel, "near_list": near_list, "far_gap": far_gap, "far_leaf": far_leaf, "par_pick": par_pick}


kernel_rate = 1.5

def kernel_block(left_pts, right_pts):
    left_wide = left_pts.astype(jnp.float32)
    right_wide = right_pts.astype(jnp.float32)
    left_sq = lax.optimization_barrier(jnp.sum(left_wide * left_wide, axis=-1))
    right_sq = lax.optimization_barrier(jnp.sum(right_wide * right_wide, axis=-1))
    inner_prod = jnp.einsum('...nd,...md->...nm', left_wide, right_wide)
    sq_dist = left_sq[..., :, None] + right_sq[..., None, :] - 2.0 * inner_prod
    return jnp.exp(-kernel_rate * sq_dist / left_pts.shape[-1])

def reference(points, charges, skel, near_list, far_gap, far_leaf, par_pick):
    leaf_pts = points.reshape(N_LEAVES, LEAF, DIM)
    leaf_chg = charges.reshape(N_LEAVES, LEAF, RHS)
    skel_pts = jnp.take_along_axis(leaf_pts, skel[:, :, None].astype(jnp.int32), axis=1)

    def basis_of(operands):
        block_pts, block_skel, block_chg = operands
        leaf_basis = kernel_block(block_pts, block_skel).astype(jnp.bfloat16)
        packed = jnp.dot(leaf_basis.T.astype(jnp.float32), block_chg.astype(jnp.float32), preferred_element_type=jnp.float32).astype(jnp.bfloat16)
        return (leaf_basis, packed)
    leaf_bases, compressed = lax.map(basis_of, (leaf_pts, skel_pts, leaf_chg))
    leaf_ids = jnp.arange(N_LEAVES, dtype=jnp.int32)
    column = leaf_ids // (N_SIB * LEAVES_DEV)
    row_index = leaf_ids // LEAVES_DEV % N_SIB
    base_ids = leaf_ids // LEAVES_DEV * LEAVES_DEV
    sources = ((column[:, None] + 1 + far_gap) % N_WIDE * N_SIB + row_index[:, None]) * LEAVES_DEV + far_leaf
    sources = sources.astype(jnp.int32)
    nbr_ids = (base_ids[:, None] + near_list).astype(jnp.int32)

    def leaf_potential(operands):
        block_pts, block_basis, block_skel, src_ids, near_ids = operands
        near_pts = leaf_pts[near_ids].reshape(NEAR * LEAF, DIM)
        near_chg = leaf_chg[near_ids].reshape(NEAR * LEAF, RHS)
        near_tiles = kernel_block(block_pts, near_pts).astype(jnp.bfloat16)
        near_sum = jnp.dot(near_tiles.astype(jnp.float32), near_chg.astype(jnp.float32), preferred_element_type=jnp.float32)
        far_pts = skel_pts[src_ids]
        far_q = compressed[src_ids]
        coupling = kernel_block(jnp.broadcast_to(block_skel, far_pts.shape), far_pts).astype(jnp.bfloat16)
        gathered = jnp.einsum('kab,kbc->ac', coupling.astype(jnp.float32), far_q.astype(jnp.float32)).astype(jnp.bfloat16)
        summed = near_sum + jnp.dot(block_basis.astype(jnp.float32), gathered.astype(jnp.float32), preferred_element_type=jnp.float32)
        return summed.astype(jnp.bfloat16)
    potential = lax.map(leaf_potential, (leaf_pts, leaf_bases, skel_pts, sources, nbr_ids))
    potential = potential.reshape(NPTS, RHS)
    grouped = skel_pts.reshape(N_WIDE, N_SIB // 2, 2, LEAVES_DEV, R, DIM)
    picks = par_pick.reshape(N_WIDE, N_SIB // 2, 2, LEAVES_DEV, HALF_R).astype(jnp.int32)
    first_skel = grouped[:, :, 0].reshape(-1, R, DIM)
    second_skel = grouped[:, :, 1].reshape(-1, R, DIM)
    first_pick = picks[:, :, 0].reshape(-1, HALF_R)
    second_pick = picks[:, :, 1].reshape(-1, HALF_R)
    root_factor = math.sqrt(2 * R)

    def merge_pair(operands):
        skel_a, skel_b, pick_a, pick_b = operands
        parent = jnp.concatenate([skel_a[pick_a], skel_b[pick_b]], axis=0)
        block_a = kernel_block(skel_a, parent)
        block_b = kernel_block(skel_b, parent)
        gram_a = jnp.dot(block_a.T, block_a, precision=lax.Precision.HIGHEST)
        gram_b = jnp.dot(block_b.T, block_b, precision=lax.Precision.HIGHEST)
        gram_sum = gram_a + gram_b + jnp.eye(R, dtype=block_a.dtype)
        lower = jnp.linalg.cholesky(gram_sum)
        out_a = root_factor * lax.linalg.triangular_solve(lower, block_a, left_side=False, lower=True, transpose_a=True)
        out_b = root_factor * lax.linalg.triangular_solve(lower, block_b, left_side=False, lower=True, transpose_a=True)
        return (out_a, out_b)
    out_a, out_b = lax.map(merge_pair, (first_skel, second_skel, first_pick, second_pick))
    out_a = out_a.reshape(N_WIDE, N_SIB // 2, LEAVES_DEV, R, R)
    out_b = out_b.reshape(N_WIDE, N_SIB // 2, LEAVES_DEV, R, R)
    transfer = jnp.stack([out_a, out_b], axis=2).reshape(N_LEAVES, R, R)
    return (potential, transfer)
```

```python
import functools
import math

import jax
import jax.numpy as jnp
from jax import lax
from jax.experimental import pallas as pl
from jax.experimental.pallas import tpu as pltpu
from jax.sharding import PartitionSpec as P

F32, BF16 = jnp.float32, jnp.bfloat16
RATE = 2.0 * 1.5 / 128 / math.log(2.0)
NN = (((1,), (0,)), ((), ()))
NT = (((1,), (1,)), ((), ()))
TN = (((0,), (0,)), ((), ()))
MESH = pl.DeviceIdType.MESH

LEAVES, HALF = 16, 8
XN, ZN = 4, 8
PANEL = 32
CHUNKS = 7
UP = [(0, 0), (0, 1), (7, 0), (7, 1), (6, 0), (6, 1), (5, 0)]
DOWN = [(0, 1), (0, 0), (1, 1), (1, 0), (2, 1), (2, 0), (3, 1)]


def mm(a, b, dims=NN):
    return lax.dot_general(a, b, dims, preferred_element_type=F32)


def squares(pts):
    wide = pts.astype(F32)
    sq = wide * wide
    high = sq.astype(BF16)
    return high, (sq - high.astype(F32)).astype(BF16)


def half_col(pts):
    high, low = squares(pts)
    ones = jnp.ones((128, 128), BF16)
    return -0.5 * (mm(high, ones) + mm(low, ones))


def half_rows(pts):
    high, low = squares(pts)
    ones = jnp.ones((16, 128), BF16)
    return (-0.5 * (mm(ones, high, NT) + mm(ones, low, NT)))[0:8]


def kernel_exp(inner, col, row):
    return jnp.exp2(RATE * (inner + (col + row)))


def three(x):
    a = x.astype(BF16)
    rest = x - a.astype(F32)
    b = rest.astype(BF16)
    return a, b, (rest - b.astype(F32)).astype(BF16)


def pick_rows(index_row, pts):
    place = lax.broadcasted_iota(jnp.int32, (pts.shape[0], index_row.shape[1]), 0)
    hot = jnp.where(place == index_row, 1.0, 0.0).astype(BF16)
    return mm(hot, pts, TN).astype(BF16)


def near_prepare(x_ref, left_ref, right_ref, g):
    pts = x_ref[g]
    n1, n2, n3 = three(half_col(pts))
    lane = lax.broadcasted_iota(jnp.int32, pts.shape, 1)
    one, zero = jnp.ones(pts.shape, BF16), jnp.zeros(pts.shape, BF16)

    def parts(at):
        rest = jnp.where(lane == at + 2, n3, zero)
        return jnp.where(lane == at, n1, jnp.where(lane == at + 1, n2, rest))

    left_ref[g, :, 0:128] = pts
    right_ref[g, :, 0:128] = pts
    left_ref[g, :, 128:256] = jnp.where((lane >= 3) & (lane < 6), one, parts(0))
    right_ref[g, :, 128:256] = jnp.where(lane < 3, one, parts(3))


def near_leaf(left_ref, right_ref, c_ref, near_ref, g):
    left = left_ref[g]
    total = None
    for k in range(near_ref.shape[1]):
        m = near_ref[g, k]
        tile = jnp.exp2(RATE * mm(left, right_ref[m], NT)).astype(BF16)
        term = mm(tile, c_ref[m])
        total = term if total is None else total + term
    return total


def build_parent(w_ref, m, sa, sb, pa, pb):
    par = jnp.concatenate([pick_rows(pa, sa), pick_rows(pb, sb)], axis=0)
    col = half_col(par)
    ea = kernel_exp(mm(par, sa, NT), col, half_rows(sa)[0:1])
    eb = kernel_exp(mm(par, sb, NT), col, half_rows(sb)[0:1])
    both = jnp.concatenate([ea, eb], axis=1)
    gram = lax.dot_general(
        both, both, NT, precision=lax.Precision.HIGHEST, preferred_element_type=F32
    )
    row = lax.broadcasted_iota(jnp.int32, (128, 128), 0)
    lane = lax.broadcasted_iota(jnp.int32, (128, 128), 1)
    w_ref[m, :, 0:128] = gram + jnp.where(row == lane, 1.0, 0.0)
    w_ref[m, :, 128:384] = both


def factor_panel(w_ref, p):
    r0, b, n = p * PANEL, PANEL, w_ref.shape[0]
    lane = lax.broadcasted_iota(jnp.int32, (1, b, 128), 2)
    row = lax.broadcasted_iota(jnp.int32, (1, b, 128), 1)
    slab = w_ref[:, r0 : r0 + b, 0:128]
    if r0:
        slab = pltpu.roll(slab, 128 - r0, 2)
    a = jnp.where(lane < b, slab, jnp.where(lane == row + b, 1.0, 0.0))
    diag = jnp.zeros((n, b, 128), F32)
    for j in range(b):
        col = jnp.broadcast_to(a[:, :, j : j + 1], (n, b, 128))
        piv = col[:, j : j + 1, :]
        top = a[:, j : j + 1, :] / piv
        diag = jnp.where(row == j, piv, diag)
        a = a - jnp.where(row > j, col, 0.0) * top
    root = lax.rsqrt(diag)
    root = root * (1.5 - 0.5 * diag * root * root)
    inv = pltpu.roll(jnp.where(lane < 2 * b, a, 0.0) * root, 128 - b, 2)
    for m in range(n):
        l1, l2, l3 = three(inv[m][:, 0:b])
        left = jnp.concatenate([l1, l1, l2, l2, l1, l3], axis=1)
        r1, r2, r3 = three(w_ref[m, r0 : r0 + b, :])
        right = jnp.concatenate([r1, r2, r1, r2, r3, r1], axis=0)
        done = mm(left, right)
        w_ref[m, r0 : r0 + b, :] = done
        if r0 + b < 128:
            d1, d2, d3 = three(done)
            right = jnp.concatenate([d1, d2, d1, d2, d3, d1], axis=0)
            left = jnp.concatenate([d1, d1, d2, d2, d1, d3], axis=0)[:, 0:128]
            change = mm(left, right, TN)
            w_ref[m, r0 + b : 128, :] -= change[r0 + b : 128]


def kernel(
    x_ref, c_ref, skel_ref, near_ref, codes_ref, pick_ref,
    pot_ref, transfer_ref,
    sf, qf, sg, lists, list_sm, sib_s, sib_pick, left, right, basis, near_sum,
    norms, tiles, h_out, h_in, h_own, w, t_keep, t_send, t_recv,
    s_send, s_recv, q_send, q_recv, x_send, x_recv, h_send, h_recv,
    l_send, l_recv, b_send, b_recv, local_sem,
):
    wide, sib = lax.axis_index("wide"), lax.axis_index("sib")
    x, z = wide // ZN, wide % ZN
    odd = sib % 2
    above, below = (x * ZN + (z + 1) % ZN, sib), (x * ZN + (z + ZN - 1) % ZN, sib)
    peers = [None] + [((x + d) % XN * ZN + z, sib) for d in range(1, XN)]
    twin = (wide, sib + 1 - 2 * odd)

    barrier = pltpu.get_barrier_semaphore()
    for other in (above, below, *peers[1:], twin):
        pl.semaphore_signal(barrier, inc=1, device_id=other, device_id_type=MESH)

    def remote(src, dst, send, recv, device):
        return pltpu.make_async_remote_copy(
            src_ref=src, dst_ref=dst, send_sem=send, recv_sem=recv,
            device_id=device, device_id_type=MESH,
        )

    def ring(buf, send, recv):
        pairs = []
        for i in range(CHUNKS):
            pair = []
            for way, (plan, device, step) in enumerate(((UP, above, ZN - 1), (DOWN, below, 1))):
                slot, half = plan[i]
                rows = pl.ds(half * HALF, HALF)
                pair.append(
                    remote(
                        buf.at[slot, rows], buf.at[(slot + step) % ZN, rows],
                        send.at[way, i], recv.at[way, i], device,
                    )
                )
            pairs.append(pair)
        return pairs

    s_ring, q_ring = ring(sf, s_send, s_recv), ring(qf, q_send, q_recv)
    x_copies = [
        remote(sf.at[0], sg.at[XN - d], x_send.at[d], x_recv.at[XN - d], peers[d])
        for d in range(1, XN)
    ]
    x_arrivals = [
        remote(sf.at[0], sg.at[d], x_send.at[d], x_recv.at[d], peers[d]) for d in range(1, XN)
    ]
    l_copies = [
        remote(codes_ref, lists.at[XN - d], l_send.at[d], l_recv.at[XN - d], peers[d])
        for d in range(1, XN)
    ]
    l_arrivals = [
        remote(codes_ref, lists.at[d], l_send.at[d], l_recv.at[d], peers[d]) for d in range(1, XN)
    ]
    h_copies = [
        remote(h_out.at[d], h_in.at[XN - d], h_send.at[d], h_recv.at[XN - d], peers[d])
        for d in range(1, XN)
    ]
    h_arrivals = [
        remote(h_out.at[d], h_in.at[d], h_send.at[d], h_recv.at[d], peers[d]) for d in range(1, XN)
    ]
    mine, theirs = odd * HALF, HALF - odd * HALF
    pick_copy = remote(pick_ref, sib_pick, b_send.at[0], b_recv.at[0], twin)
    sib_copy = remote(sf.at[0, pl.ds(theirs, HALF)], sib_s, b_send.at[1], b_recv.at[1], twin)
    t_copy = remote(t_send, t_recv, b_send.at[2], b_recv.at[2], twin)

    def forward(copies, i):
        for way in (0, 1):
            copies[i - 2][way].wait_recv()
            copies[i][way].start()

    def skeleton(g):
        sf[0, g] = pick_rows(skel_ref[pl.ds(g, 1), :], x_ref[g])

    @pl.loop(0, HALF // 2)
    def _(i):
        skeleton(2 * i)
        skeleton(2 * i + 1)

    pl.semaphore_wait(barrier, 6)
    s_ring[0][0].start()
    s_ring[1][1].start()
    pick_copy.start()
    for copy in l_copies:
        copy.start()

    @pl.loop(HALF // 2, HALF)
    def _(i):
        skeleton(2 * i)
        skeleton(2 * i + 1)

    s_ring[0][1].start()
    s_ring[1][0].start()
    sib_copy.start()
    for copy in x_copies:
        copy.start()

    def compress(g):
        pts, skel_pts = x_ref[g], sf[0, g]
        block = kernel_exp(mm(pts, skel_pts, NT), half_col(pts), half_rows(skel_pts)[0:1])
        block = block.astype(BF16)
        basis[g] = block
        qf[0, g] = mm(block, c_ref[g], TN).astype(BF16)

    def bases(first, last):
        @pl.loop(first // 2, last // 2)
        def _(i):
            compress(2 * i)
            compress(2 * i + 1)

    bases(0, 8)
    forward(s_ring, 2)
    bases(8, 16)
    forward(s_ring, 3)
    for i in (0, 1):
        for way in (0, 1):
            q_ring[i][way].start()

    @pl.loop(0, LEAVES)
    def _(g):
        near_prepare(x_ref, left, right, g)

    def near(first, last):
        @pl.loop(first, last)
        def _(g):
            near_sum[g] = near_leaf(left, right, c_ref, near_ref, g)

    near(0, 4)
    forward(s_ring, 4)
    near(4, 8)
    forward(q_ring, 2)
    near(8, 12)
    forward(s_ring, 5)
    near(12, 16)
    forward(q_ring, 3)

    pick_copy.wait_recv()
    sib_copy.wait_recv()

    @pl.loop(0, HALF // 2)
    def _(i):
        for m in (2 * i, 2 * i + 1):
            own, other = sf[0, mine + m], sib_s[m]
            own_pick = pick_ref[pl.ds(mine + m, 1), 0:64]
            other_pick = sib_pick[pl.ds(mine + m, 1), 0:64]
            build_parent(
                w, m,
                jnp.where(odd == 1, other, own), jnp.where(odd == 1, own, other),
                jnp.where(odd == 1, other_pick, own_pick),
                jnp.where(odd == 1, own_pick, other_pick),
            )

    forward(s_ring, 6)
    factor_panel(w, 0)
    forward(q_ring, 4)
    factor_panel(w, 1)
    factor_panel(w, 2)
    forward(q_ring, 5)
    factor_panel(w, 3)

    @pl.loop(0, HALF)
    def _(m):
        ta = w[m, :, 128:256].T * 16.0
        tb = w[m, :, 256:384].T * 16.0
        t_keep[m] = jnp.where(odd == 1, tb, ta)
        t_send[m] = jnp.where(odd == 1, ta, tb)

    t_copy.start()
    keep_copy = pltpu.make_async_copy(t_keep, transfer_ref.at[pl.ds(mine, HALF)], local_sem.at[0])
    keep_copy.start()

    for copy in l_arrivals:
        copy.wait_recv()
    list_copies = [
        pltpu.make_async_copy(codes_ref if d == 0 else lists.at[d], list_sm.at[d], local_sem.at[1 + d])
        for d in range(XN)
    ]
    for copy in list_copies:
        copy.start()
    for i in (5, 6):
        for way in (0, 1):
            s_ring[i][way].wait_recv()
    for copy in x_arrivals:
        copy.wait_recv()
    for copy in list_copies:
        copy.wait()

    @pl.loop(0, ZN * LEAVES // 4)
    def _(i):
        for f in range(4):
            norms[4 * i + f] = half_rows(sf[i // 4, i % 4 * 4 + f])

    def entry(d, g, k):
        code = list_sm[d, 0, g * 4 + k]
        ahead = 1 + (code >> 4)
        there = ((z + ahead >> 3) + d & XN - 1) == 0
        return there, (ahead & ZN - 1) * LEAVES + (code & LEAVES - 1)

    def couple(d):
        @pl.loop(0, LEAVES)
        def _(g):
            pts = sf[0, g] if d == 0 else sg[d, g]
            col = half_col(pts)
            for k in range(4):
                there, f = entry(d, g, k)
                row = norms[f][0:1] + jnp.where(there, 0.0, -1e30)
                inner = mm(pts, sf[f // LEAVES, f % LEAVES], NT)
                tiles[d, g, :, k * 128 : (k + 1) * 128] = kernel_exp(inner, col, row).astype(BF16)

    couple(2)
    couple(1)
    forward(q_ring, 6)
    couple(3)
    couple(0)

    for i in (5, 6):
        for way in (0, 1):
            q_ring[i][way].wait_recv()

    def partial(d, out):
        @pl.loop(0, LEAVES)
        def _(g):
            total = None
            for k in range(4):
                _, f = entry(d, g, k)
                term = mm(tiles[d, g, :, k * 128 : (k + 1) * 128], qf[f // LEAVES, f % LEAVES])
                total = term if total is None else total + term
            out(g, total)

    for d in (2, 1, 3):

        def put(g, total, d=d):
            h_out[d, g] = total.astype(BF16)

        partial(d, put)
        h_copies[d - 1].start()

    def put_own(g, total):
        h_own[g] = total

    partial(0, put_own)
    for copy in h_arrivals:
        copy.wait_recv()

    @pl.loop(0, LEAVES // 2)
    def _(i):
        for g in (2 * i, 2 * i + 1):
            total = h_own[g]
            for d in range(1, XN):
                total = total + h_in[d, g].astype(F32)
            value = near_sum[g] + mm(basis[g], total.astype(BF16))
            pot_ref[g] = value.astype(BF16)

    t_copy.wait_recv()
    other_copy = pltpu.make_async_copy(
        t_recv, transfer_ref.at[pl.ds(theirs, HALF)], local_sem.at[1 + XN]
    )
    other_copy.start()
    for copies in (*s_ring, *q_ring, x_copies, l_copies, h_copies, (pick_copy, sib_copy, t_copy)):
        for copy in copies:
            copy.wait_send()
    keep_copy.wait()
    other_copy.wait()


def body(points, charges, skel, near_list, far_gap, far_leaf, par_pick):
    x = points.reshape(LEAVES, 256, 128)
    c = charges.reshape(LEAVES, 256, 128)
    codes = (far_gap * LEAVES + far_leaf).reshape(1, 64)
    codes = jnp.pad(codes, ((0, 7), (0, 64)))
    pick = jnp.pad(par_pick, ((0, 0), (0, 64)))
    vmem = pl.BlockSpec(memory_space=pltpu.VMEM)
    smem = pl.BlockSpec(memory_space=pltpu.SMEM)
    block = (LEAVES, 128, 128)
    pot, transfer = pl.pallas_call(
        kernel,
        out_shape=(
            jax.ShapeDtypeStruct((LEAVES, 256, 128), BF16),
            jax.ShapeDtypeStruct((LEAVES, 128, 128), F32),
        ),
        in_specs=[vmem, vmem, vmem, smem, vmem, vmem],
        out_specs=(vmem, pl.BlockSpec(memory_space=pl.ANY)),
        scratch_shapes=[
            pltpu.VMEM((ZN, *block), BF16),
            pltpu.VMEM((ZN, *block), BF16),
            pltpu.VMEM((XN, *block), BF16),
            pltpu.VMEM((XN, 8, 128), jnp.int32),
            pltpu.SMEM((XN, 8, 128), jnp.int32),
            pltpu.VMEM((HALF, 128, 128), BF16),
            pltpu.VMEM((LEAVES, 128), jnp.int32),
            pltpu.VMEM((LEAVES, 256, 256), BF16),
            pltpu.VMEM((LEAVES, 256, 256), BF16),
            pltpu.VMEM((LEAVES, 256, 128), BF16),
            pltpu.VMEM((LEAVES, 256, 128), F32),
            pltpu.VMEM((ZN * LEAVES, 8, 128), F32),
            pltpu.VMEM((XN, LEAVES, 128, 512), BF16),
            pltpu.VMEM((XN, *block), BF16),
            pltpu.VMEM((XN, *block), BF16),
            pltpu.VMEM(block, F32),
            pltpu.VMEM((HALF, 128, 384), F32),
            pltpu.VMEM((HALF, 128, 128), F32),
            pltpu.VMEM((HALF, 128, 128), F32),
            pltpu.VMEM((HALF, 128, 128), F32),
            pltpu.SemaphoreType.DMA((2, CHUNKS)),
            pltpu.SemaphoreType.DMA((2, CHUNKS)),
            pltpu.SemaphoreType.DMA((2, CHUNKS)),
            pltpu.SemaphoreType.DMA((2, CHUNKS)),
            pltpu.SemaphoreType.DMA((XN,)),
            pltpu.SemaphoreType.DMA((XN,)),
            pltpu.SemaphoreType.DMA((XN,)),
            pltpu.SemaphoreType.DMA((XN,)),
            pltpu.SemaphoreType.DMA((XN,)),
            pltpu.SemaphoreType.DMA((XN,)),
            pltpu.SemaphoreType.DMA((3,)),
            pltpu.SemaphoreType.DMA((3,)),
            pltpu.SemaphoreType.DMA((2 + XN,)),
        ],
        compiler_params=pltpu.CompilerParams(
            collective_id=0, has_side_effects=True, vmem_limit_bytes=56 << 20
        ),
        cost_estimate=pl.CostEstimate(flops=5_000_000_000, bytes_accessed=5_000_000, transcendentals=10_000_000),
    )(x, c, skel, near_list, codes, pick)
    return pot.reshape(LEAVES * 256, 128), transfer


def solution(mesh):
    placed = P(("wide", "sib"), None)
    return jax.shard_map(
        body,
        mesh=mesh,
        in_specs=(placed,) * 7,
        out_specs=(placed, P(("wide", "sib"), None, None)),
        check_vma=False,
    )
```

```python
import functools
import math

import jax
import jax.numpy as jnp
from jax import lax
from jax.experimental import pallas as pl
from jax.experimental.pallas import tpu as pltpu
from jax.sharding import PartitionSpec as P

F32, BF16 = jnp.float32, jnp.bfloat16
RATE = 2.0 * 1.5 / 128 / math.log(2.0)
NN = (((1,), (0,)), ((), ()))
NT = (((1,), (1,)), ((), ()))
TN = (((0,), (0,)), ((), ()))
MESH = pl.DeviceIdType.MESH

LEAVES, HALF = 16, 8
XN, ZN = 4, 8
PANEL = 32
CHUNKS = 7
PARTS, STARTS, COLS = 2, (0, 64), (64, 64)
UP = [(0, 0), (0, 1), (7, 0), (7, 1), (6, 0), (6, 1), (5, 0)]
DOWN = [(0, 1), (0, 0), (1, 1), (1, 0), (2, 1), (2, 0), (3, 1)]


def mm(a, b, dims=NN):
    return lax.dot_general(a, b, dims, preferred_element_type=F32)


def squares(pts):
    wide = pts.astype(F32)
    sq = wide * wide
    high = sq.astype(BF16)
    return high, (sq - high.astype(F32)).astype(BF16)


def half_col(pts):
    high, low = squares(pts)
    ones = jnp.ones((128, 128), BF16)
    return -0.5 * (mm(high, ones) + mm(low, ones))


def half_rows(pts):
    high, low = squares(pts)
    ones = jnp.ones((16, 128), BF16)
    return (-0.5 * (mm(ones, high, NT) + mm(ones, low, NT)))[0:8]


def kernel_exp(inner, col, row):
    return jnp.exp2(RATE * (inner + (col + row)))


def three(x):
    a = x.astype(BF16)
    rest = x - a.astype(F32)
    b = rest.astype(BF16)
    return a, b, (rest - b.astype(F32)).astype(BF16)


def pick_rows(index_row, pts):
    place = lax.broadcasted_iota(jnp.int32, (pts.shape[0], index_row.shape[1]), 0)
    hot = jnp.where(place == index_row, 1.0, 0.0).astype(BF16)
    return mm(hot, pts, TN).astype(BF16)


def near_prepare(x_ref, left_ref, right_ref, g):
    pts = x_ref[g]
    n1, n2, n3 = three(half_col(pts))
    lane = lax.broadcasted_iota(jnp.int32, pts.shape, 1)
    one, zero = jnp.ones(pts.shape, BF16), jnp.zeros(pts.shape, BF16)

    def parts(at):
        rest = jnp.where(lane == at + 2, n3, zero)
        return jnp.where(lane == at, n1, jnp.where(lane == at + 1, n2, rest))

    left_ref[g, :, 0:128] = pts
    right_ref[g, :, 0:128] = pts
    left_ref[g, :, 128:256] = jnp.where((lane >= 3) & (lane < 6), one, parts(0))
    right_ref[g, :, 128:256] = jnp.where(lane < 3, one, parts(3))


def near_leaf(left_ref, right_ref, c_ref, near_ref, g):
    left = left_ref[g]
    total = None
    for k in range(near_ref.shape[1]):
        m = near_ref[g, k]
        tile = jnp.exp2(RATE * mm(left, right_ref[m], NT)).astype(BF16)
        term = mm(tile, c_ref[m])
        total = term if total is None else total + term
    return total


def build_parent(w_ref, m, sa, sb, pa, pb):
    par = jnp.concatenate([pick_rows(pa, sa), pick_rows(pb, sb)], axis=0)
    col = half_col(par)
    ea = kernel_exp(mm(par, sa, NT), col, half_rows(sa)[0:1])
    eb = kernel_exp(mm(par, sb, NT), col, half_rows(sb)[0:1])
    both = jnp.concatenate([ea, eb], axis=1)
    gram = lax.dot_general(
        both, both, NT, precision=lax.Precision.HIGHEST, preferred_element_type=F32
    )
    row = lax.broadcasted_iota(jnp.int32, (128, 128), 0)
    lane = lax.broadcasted_iota(jnp.int32, (128, 128), 1)
    w_ref[m, :, 0:128] = gram + jnp.where(row == lane, 1.0, 0.0)
    w_ref[m, :, 128:384] = both


def factor_panel(w_ref, p):
    r0, b, n = p * PANEL, PANEL, w_ref.shape[0]
    lane = lax.broadcasted_iota(jnp.int32, (1, b, 128), 2)
    row = lax.broadcasted_iota(jnp.int32, (1, b, 128), 1)
    slab = w_ref[:, r0 : r0 + b, 0:128]
    if r0:
        slab = pltpu.roll(slab, 128 - r0, 2)
    a = jnp.where(lane < b, slab, jnp.where(lane == row + b, 1.0, 0.0))
    diag = jnp.zeros((n, b, 128), F32)
    for j in range(b):
        col = jnp.broadcast_to(a[:, :, j : j + 1], (n, b, 128))
        piv = col[:, j : j + 1, :]
        top = a[:, j : j + 1, :] / piv
        diag = jnp.where(row == j, piv, diag)
        a = a - jnp.where(row > j, col, 0.0) * top
    root = lax.rsqrt(diag)
    root = root * (1.5 - 0.5 * diag * root * root)
    inv = pltpu.roll(jnp.where(lane < 2 * b, a, 0.0) * root, 128 - b, 2)
    for m in range(n):
        l1, l2, l3 = three(inv[m][:, 0:b])
        left = jnp.concatenate([l1, l1, l2, l2, l1, l3], axis=1)
        r1, r2, r3 = three(w_ref[m, r0 : r0 + b, :])
        right = jnp.concatenate([r1, r2, r1, r2, r3, r1], axis=0)
        done = mm(left, right)
        w_ref[m, r0 : r0 + b, :] = done
        if r0 + b < 128:
            d1, d2, d3 = three(done)
            right = jnp.concatenate([d1, d2, d1, d2, d3, d1], axis=0)
            left = jnp.concatenate([d1, d1, d2, d2, d1, d3], axis=0)[:, 0:128]
            change = mm(left, right, TN)
            w_ref[m, r0 + b : 128, :] -= change[r0 + b : 128]


def kernel(
    x_ref, c_ref, skel_ref, near_ref, codes_ref, pick_ref,
    pot_ref, transfer_ref,
    sf, qf, sg, lists, list_sm, sib_s, sib_pick, left, right, basis, near_sum,
    norms, tiles, h_out, h_far, h_in, h_own, w, t_send, t_recv,
    s_send, s_recv, q_send, q_recv, n_send, n_recv, x_send, x_recv, f_send, f_recv,
    h_send, h_recv, l_send, l_recv, b_send, b_recv, local_sem,
):
    wide, sib = lax.axis_index("wide"), lax.axis_index("sib")
    x, z = wide // ZN, wide % ZN
    odd = sib % 2
    above, below = (x * ZN + (z + 1) % ZN, sib), (x * ZN + (z + ZN - 1) % ZN, sib)
    peers = [None] + [((x + d) % XN * ZN + z, sib) for d in range(1, XN)]
    twin = (wide, sib + 1 - 2 * odd)

    barrier = pltpu.get_barrier_semaphore()
    for other in (above, below, *peers[1:], twin):
        pl.semaphore_signal(barrier, inc=1, device_id=other, device_id_type=MESH)

    def remote(src, dst, send, recv, device):
        return pltpu.make_async_remote_copy(
            src_ref=src, dst_ref=dst, send_sem=send, recv_sem=recv,
            device_id=device, device_id_type=MESH,
        )

    def ring(buf, send, recv):
        pairs = []
        for i in range(CHUNKS):
            pair = []
            for way, (plan, device, step) in enumerate(((UP, above, ZN - 1), (DOWN, below, 1))):
                slot, half = plan[i]
                rows = pl.ds(half * HALF, HALF)
                pair.append(
                    remote(
                        buf.at[slot, rows], buf.at[(slot + step) % ZN, rows],
                        send.at[way, i], recv.at[way, i], device,
                    )
                )
            pairs.append(pair)
        return pairs

    s_ring = ring(sf, s_send, s_recv)
    q_ring = [ring(qf[p], q_send.at[p], q_recv.at[p]) for p in range(PARTS)]
    n_ring = []
    for hop in range(4):
        up, down = (ZN - hop) % ZN, hop
        pair = [
            remote(norms.at[up], norms.at[up - 1 if hop else ZN - 1],
                   n_send.at[0, hop], n_recv.at[0, hop], above)
        ]
        if hop < 3:
            pair.append(
                remote(norms.at[down], norms.at[down + 1],
                       n_send.at[1, hop], n_recv.at[1, hop], below)
            )
        n_ring.append(pair)
    x_copies = [
        remote(sf.at[0], sg.at[XN - d], x_send.at[d], x_recv.at[XN - d], peers[d])
        for d in range(1, XN)
    ]
    x_arrivals = [
        remote(sf.at[0], sg.at[d], x_send.at[d], x_recv.at[d], peers[d]) for d in range(1, XN)
    ]
    l_copies = [
        remote(codes_ref, lists.at[XN - d], l_send.at[d], l_recv.at[XN - d], peers[d])
        for d in range(1, XN)
    ]
    l_arrivals = [
        remote(codes_ref, lists.at[d], l_send.at[d], l_recv.at[d], peers[d]) for d in range(1, XN)
    ]
    f_copies = [
        [
            remote(h_out[p].at[2, pl.ds(way * HALF, HALF)], h_far[p].at[way],
                   f_send.at[p, way], f_recv.at[p, way], peers[1 + 2 * way])
            for way in (0, 1)
        ]
        for p in range(PARTS)
    ]
    h_copies = [
        [
            remote(h_out[p].at[1 + 2 * way], h_in[p].at[way],
                   h_send.at[p, way], h_recv.at[p, way], peers[1 + 2 * way])
            for way in (0, 1)
        ]
        for p in range(PARTS)
    ]
    mine, theirs = odd * HALF, HALF - odd * HALF
    pick_copy = remote(pick_ref, sib_pick, b_send.at[0], b_recv.at[0], twin)
    sib_copy = remote(sf.at[0, pl.ds(theirs, HALF)], sib_s, b_send.at[1], b_recv.at[1], twin)
    t_copy = remote(t_send, t_recv, b_send.at[2], b_recv.at[2], twin)

    def start(copies, *chunks):
        for i in chunks:
            for way in (0, 1):
                if i >= 2:
                    copies[i - 2][way].wait_recv()
                copies[i][way].start()

    def start_norms(hop):
        for way, copy in enumerate(n_ring[hop]):
            if hop:
                n_ring[hop - 1][way].wait_recv()
            copy.start()

    def skeleton(g):
        sf[0, g] = pick_rows(skel_ref[pl.ds(g, 1), :], x_ref[g])

    @pl.loop(0, HALF // 2)
    def _(i):
        skeleton(2 * i)
        skeleton(2 * i + 1)

    pl.semaphore_wait(barrier, 6)
    s_ring[0][0].start()
    s_ring[1][1].start()
    pick_copy.start()
    for copy in l_copies:
        copy.start()

    @pl.loop(HALF // 2, HALF)
    def _(i):
        skeleton(2 * i)
        skeleton(2 * i + 1)

    s_ring[0][1].start()
    s_ring[1][0].start()
    sib_copy.start()
    for copy in x_copies:
        copy.start()

    def compress(g):
        pts, skel_pts = x_ref[g], sf[0, g]
        row = half_rows(skel_pts)[0:1]
        norms[0, pl.ds(g, 1), :] = row
        block = kernel_exp(mm(pts, skel_pts, NT), half_col(pts), row).astype(BF16)
        basis[g] = block
        squeezed = mm(c_ref[g], block, TN).astype(BF16)
        for p in range(PARTS):
            qf[p][0, g] = squeezed[STARTS[p] : STARTS[p] + COLS[p]]

    @pl.loop(0, LEAVES // 2, unroll=2)
    def _(i):
        compress(2 * i)
        compress(2 * i + 1)

    start(q_ring[0], 0, 1)
    start_norms(0)

    @pl.loop(0, LEAVES, unroll=4)
    def _(g):
        near_prepare(x_ref, left, right, g)

    def near(first, last):
        @pl.loop(first, last, unroll=2)
        def _(g):
            near_sum[g] = near_leaf(left, right, c_ref, near_ref, g)

    near(0, 6)
    start(s_ring, 2)
    near(6, 8)
    start(s_ring, 3)
    near(8, 12)
    start(q_ring[0], 2)
    near(12, 14)
    start(q_ring[0], 3)
    start_norms(1)
    near(14, 16)
    start(s_ring, 4)
    start(q_ring[1], 0, 1)

    pick_copy.wait_recv()
    sib_copy.wait_recv()

    @pl.loop(0, HALF // 2)
    def _(i):
        for m in (2 * i, 2 * i + 1):
            own, other = sf[0, mine + m], sib_s[m]
            own_pick = pick_ref[pl.ds(mine + m, 1), :]
            other_pick = sib_pick[pl.ds(mine + m, 1), :]
            build_parent(
                w, m,
                jnp.where(odd == 1, other, own), jnp.where(odd == 1, own, other),
                jnp.where(odd == 1, other_pick, own_pick),
                jnp.where(odd == 1, own_pick, other_pick),
            )

    start(s_ring, 5)
    start_norms(2)
    factor_panel(w, 0)
    start(q_ring[0], 4)
    start(s_ring, 6)
    start_norms(3)
    factor_panel(w, 1)
    start(q_ring[0], 5)
    start(q_ring[1], 2)
    factor_panel(w, 2)
    start(q_ring[0], 6)
    start(q_ring[1], 3)
    factor_panel(w, 3)

    @pl.loop(0, HALF)
    def _(m):
        ta = w[m, :, 128:256].T * 16.0
        tb = w[m, :, 256:384].T * 16.0
        transfer_ref[mine + m] = jnp.where(odd == 1, tb, ta)
        t_send[m] = jnp.where(odd == 1, ta, tb)

    t_copy.start()

    for copy in l_arrivals:
        copy.wait_recv()
    list_copies = [
        pltpu.make_async_copy(codes_ref if d == 0 else lists.at[d], list_sm.at[d], local_sem.at[d])
        for d in range(XN)
    ]
    for copy in list_copies:
        copy.start()
    for copy in (*s_ring[5], *s_ring[6], *x_arrivals, n_ring[2][1], n_ring[3][0]):
        copy.wait_recv()
    for copy in list_copies:
        copy.wait()

    def entry(d, g, k):
        code = list_sm[d, 0, g * 4 + k]
        ahead = 1 + (code >> 4)
        there = ((z + ahead >> 3) + d & XN - 1) == 0
        return there, ahead & ZN - 1, code & LEAVES - 1

    def couple(d):
        @pl.loop(0, LEAVES, unroll=4)
        def _(g):
            pts = sf[0, g] if d == 0 else sg[d, g]
            col = half_col(pts)
            rows, named = [], []
            for k in range(4):
                there, slot, leaf = entry(d, g, k)
                rows.append(norms[slot, pl.ds(leaf, 1), :] + jnp.where(there, 0.0, -1e30))
                named.append(sf[slot, leaf])
            inner = mm(pts, jnp.concatenate(named, axis=0), NT)
            col = jnp.concatenate([col] * 4, axis=1)
            tiles[d, g] = kernel_exp(inner, col, jnp.concatenate(rows, axis=1)).astype(BF16)

    couple(2)
    start(q_ring[1], 4)
    couple(1)
    start(q_ring[1], 5)
    couple(3)
    couple(0)

    def partial(p, d, first, last, out):
        @pl.loop(first, last, unroll=8)
        def _(g):
            named = []
            for k in range(4):
                _, slot, leaf = entry(d, g, k)
                named.append(qf[p][slot, leaf])
            out(g, mm(jnp.concatenate(named, axis=1), tiles[d, g], NT))

    def far_part(p):
        for way in (0, 1):
            for i in (5, 6):
                q_ring[p][i][way].wait_recv()

        def put_far(g, total):
            h_out[p][2, g] = total.astype(BF16)

        def put_own(g, total):
            h_own[p][g] = total

        partial(p, 2, 0, LEAVES, put_far)
        for way in (0, 1):
            f_copies[p][way].start()
        if p == 0:
            start(q_ring[1], 6)
        partial(p, 0, 0, LEAVES, put_own)
        for way in (0, 1):
            d = 1 + 2 * way

            def put(g, total, d=d):
                h_out[p][d, g] = total.astype(BF16)

            def put_sum(g, total, d=d, way=way):
                total = total + h_far[p][way, g - way * HALF].astype(F32)
                h_out[p][d, g] = total.astype(BF16)

            partial(p, d, HALF - way * HALF, LEAVES - way * HALF, put)
            f_copies[p][way].wait_recv()
            partial(p, d, way * HALF, HALF + way * HALF, put_sum)
            h_copies[p][way].start()

    far_part(0)

    t_copy.wait_recv()

    @pl.loop(0, HALF)
    def _(m):
        transfer_ref[theirs + m] = t_recv[m]

    far_part(1)
    for copies in h_copies:
        for copy in copies:
            copy.wait_recv()

    @pl.loop(0, LEAVES // 2)
    def _(i):
        for g in (2 * i, 2 * i + 1):
            total = []
            for p in range(PARTS):
                share = h_own[p][g] + h_in[p][0, g].astype(F32) + h_in[p][1, g].astype(F32)
                total.append(share.astype(BF16))
            value = near_sum[g] + mm(basis[g], jnp.concatenate(total, axis=0), NT)
            pot_ref[g] = value.astype(BF16)

    sent = [*s_ring, *n_ring, x_copies, l_copies, *f_copies, *h_copies]
    for p in range(PARTS):
        sent.extend(q_ring[p])
    for copies in (*sent, (pick_copy, sib_copy, t_copy)):
        for copy in copies:
            copy.wait_send()


def body(points, charges, skel, near_list, far_gap, far_leaf, par_pick):
    x = points.reshape(LEAVES, 256, 128)
    c = charges.reshape(LEAVES, 256, 128)
    codes = (far_gap * LEAVES + far_leaf).reshape(1, 64)
    codes = jnp.pad(codes, ((0, 7), (0, 64)))
    vmem = pl.BlockSpec(memory_space=pltpu.VMEM)
    smem = pl.BlockSpec(memory_space=pltpu.SMEM)
    block = (LEAVES, 128, 128)
    pot, transfer = pl.pallas_call(
        kernel,
        out_shape=(
            jax.ShapeDtypeStruct((LEAVES, 256, 128), BF16),
            jax.ShapeDtypeStruct((LEAVES, 128, 128), F32),
        ),
        in_specs=[vmem, vmem, vmem, smem, vmem, vmem],
        out_specs=(vmem, vmem),
        scratch_shapes=[
            pltpu.VMEM((ZN, *block), BF16),
            [pltpu.VMEM((ZN, LEAVES, n, 128), BF16) for n in COLS],
            pltpu.VMEM((XN, *block), BF16),
            pltpu.VMEM((XN, 8, 128), jnp.int32),
            pltpu.SMEM((XN, 8, 128), jnp.int32),
            pltpu.VMEM((HALF, 128, 128), BF16),
            pltpu.VMEM((LEAVES, 64), jnp.int32),
            pltpu.VMEM((LEAVES, 256, 256), BF16),
            pltpu.VMEM((LEAVES, 256, 256), BF16),
            pltpu.VMEM((LEAVES, 256, 128), BF16),
            pltpu.VMEM((LEAVES, 256, 128), F32),
            pltpu.VMEM((ZN, LEAVES, 128), F32),
            pltpu.VMEM((XN, LEAVES, 128, 512), BF16),
            [pltpu.VMEM((XN, LEAVES, n, 128), BF16) for n in COLS],
            [pltpu.VMEM((2, HALF, n, 128), BF16) for n in COLS],
            [pltpu.VMEM((2, LEAVES, n, 128), BF16) for n in COLS],
            [pltpu.VMEM((LEAVES, n, 128), F32) for n in COLS],
            pltpu.VMEM((HALF, 128, 384), F32),
            pltpu.VMEM((HALF, 128, 128), F32),
            pltpu.VMEM((HALF, 128, 128), F32),
            pltpu.SemaphoreType.DMA((2, CHUNKS)),
            pltpu.SemaphoreType.DMA((2, CHUNKS)),
            pltpu.SemaphoreType.DMA((PARTS, 2, CHUNKS)),
            pltpu.SemaphoreType.DMA((PARTS, 2, CHUNKS)),
            pltpu.SemaphoreType.DMA((2, 4)),
            pltpu.SemaphoreType.DMA((2, 4)),
            pltpu.SemaphoreType.DMA((XN,)),
            pltpu.SemaphoreType.DMA((XN,)),
            pltpu.SemaphoreType.DMA((PARTS, 2)),
            pltpu.SemaphoreType.DMA((PARTS, 2)),
            pltpu.SemaphoreType.DMA((PARTS, 2)),
            pltpu.SemaphoreType.DMA((PARTS, 2)),
            pltpu.SemaphoreType.DMA((XN,)),
            pltpu.SemaphoreType.DMA((XN,)),
            pltpu.SemaphoreType.DMA((3,)),
            pltpu.SemaphoreType.DMA((3,)),
            pltpu.SemaphoreType.DMA((XN,)),
        ],
        compiler_params=pltpu.CompilerParams(
            collective_id=0, has_side_effects=True, vmem_limit_bytes=56 << 20
        ),
        cost_estimate=pl.CostEstimate(flops=5_000_000_000, bytes_accessed=5_000_000, transcendentals=10_000_000),
    )(x, c, skel, near_list, codes, par_pick)
    return pot.reshape(LEAVES * 256, 128), transfer


def solution(mesh):
    placed = P(("wide", "sib"), None)
    return jax.shard_map(
        body,
        mesh=mesh,
        in_specs=(placed,) * 7,
        out_specs=(placed, P(("wide", "sib"), None, None)),
        check_vma=False,
    )
```

```python
import functools
import math

import jax
import jax.numpy as jnp
from jax import lax
from jax.experimental import pallas as pl
from jax.experimental.pallas import tpu as pltpu
from jax.sharding import PartitionSpec as P

F32, BF16 = jnp.float32, jnp.bfloat16
RATE = 2.0 * 1.5 / 128 / math.log(2.0)
NN = (((1,), (0,)), ((), ()))
NT = (((1,), (1,)), ((), ()))
TN = (((0,), (0,)), ((), ()))
MESH = pl.DeviceIdType.MESH

LEAVES, HALF = 16, 8
XN, ZN = 4, 8
PANEL = 32
CHUNKS = 7
PARTS, STARTS, COLS = 2, (0, 64), (64, 64)
UP = [(0, 0), (0, 1), (7, 0), (7, 1), (6, 0), (6, 1), (5, 0)]
DOWN = [(0, 1), (0, 0), (1, 1), (1, 0), (2, 1), (2, 0), (3, 1)]


def mm(a, b, dims=NN):
    return lax.dot_general(a, b, dims, preferred_element_type=F32)


def squares(pts):
    wide = pts.astype(F32)
    sq = wide * wide
    high = sq.astype(BF16)
    return high, (sq - high.astype(F32)).astype(BF16)


def half_col(pts):
    high, low = squares(pts)
    ones = jnp.ones((128, 128), BF16)
    return -0.5 * (mm(high, ones) + mm(low, ones))


def half_rows(pts):
    high, low = squares(pts)
    ones = jnp.ones((16, 128), BF16)
    return (-0.5 * (mm(ones, high, NT) + mm(ones, low, NT)))[0:8]


def kernel_exp(inner, col, row):
    return jnp.exp2(RATE * (inner + (col + row)))


def three(x):
    a = x.astype(BF16)
    rest = x - a.astype(F32)
    b = rest.astype(BF16)
    return a, b, (rest - b.astype(F32)).astype(BF16)


def pick_rows(index_row, pts):
    place = lax.broadcasted_iota(jnp.int32, (pts.shape[0], index_row.shape[1]), 0)
    hot = jnp.where(place == index_row, 1.0, 0.0).astype(BF16)
    return mm(hot, pts, TN).astype(BF16)


def near_prepare(x_ref, left_ref, right_ref, g):
    pts = x_ref[g]
    n1, n2, n3 = three(half_col(pts))
    lane = lax.broadcasted_iota(jnp.int32, pts.shape, 1)
    one, zero = jnp.ones(pts.shape, BF16), jnp.zeros(pts.shape, BF16)

    def parts(at):
        rest = jnp.where(lane == at + 2, n3, zero)
        return jnp.where(lane == at, n1, jnp.where(lane == at + 1, n2, rest))

    left_ref[g, :, 0:128] = pts
    right_ref[g, :, 0:128] = pts
    left_ref[g, :, 128:256] = jnp.where((lane >= 3) & (lane < 6), one, parts(0))
    right_ref[g, :, 128:256] = jnp.where(lane < 3, one, parts(3))


def near_leaf(left_ref, right_ref, c_ref, near_ref, g):
    left = left_ref[g]
    total = None
    for k in range(near_ref.shape[1]):
        m = near_ref[g, k]
        tile = jnp.exp2(RATE * mm(left, right_ref[m], NT)).astype(BF16)
        term = mm(tile, c_ref[m])
        total = term if total is None else total + term
    return total


def build_parent(w_ref, m, sa, sb, pa, pb):
    par = jnp.concatenate([pick_rows(pa, sa), pick_rows(pb, sb)], axis=0)
    col = half_col(par)
    ea = kernel_exp(mm(par, sa, NT), col, half_rows(sa)[0:1])
    eb = kernel_exp(mm(par, sb, NT), col, half_rows(sb)[0:1])
    both = jnp.concatenate([ea, eb], axis=1)
    gram = lax.dot_general(
        both, both, NT, precision=lax.Precision.HIGHEST, preferred_element_type=F32
    )
    row = lax.broadcasted_iota(jnp.int32, (128, 128), 0)
    lane = lax.broadcasted_iota(jnp.int32, (128, 128), 1)
    w_ref[m, :, 0:128] = gram + jnp.where(row == lane, 1.0, 0.0)
    w_ref[m, :, 128:384] = both


def factor_panel(w_ref, p):
    r0, b, n = p * PANEL, PANEL, w_ref.shape[0]
    lane = lax.broadcasted_iota(jnp.int32, (1, b, 128), 2)
    row = lax.broadcasted_iota(jnp.int32, (1, b, 128), 1)
    slab = w_ref[:, r0 : r0 + b, 0:128]
    if r0:
        slab = pltpu.roll(slab, 128 - r0, 2)
    a = jnp.where(lane < b, slab, jnp.where(lane == row + b, 1.0, 0.0))
    diag = jnp.zeros((n, b, 128), F32)
    for j in range(b):
        col = jnp.broadcast_to(a[:, :, j : j + 1], (n, b, 128))
        piv = col[:, j : j + 1, :]
        top = a[:, j : j + 1, :] / piv
        diag = jnp.where(row == j, piv, diag)
        a = a - jnp.where(row > j, col, 0.0) * top
    root = lax.rsqrt(diag)
    root = root * (1.5 - 0.5 * diag * root * root)
    inv = pltpu.roll(jnp.where(lane < 2 * b, a, 0.0) * root, 128 - b, 2)
    for m in range(n):
        l1, l2, l3 = three(inv[m][:, 0:b])
        left = jnp.concatenate([l1, l1, l2, l2, l1, l3], axis=1)
        r1, r2, r3 = three(w_ref[m, r0 : r0 + b, :])
        right = jnp.concatenate([r1, r2, r1, r2, r3, r1], axis=0)
        done = mm(left, right)
        w_ref[m, r0 : r0 + b, :] = done
        if r0 + b < 128:
            d1, d2, d3 = three(done)
            right = jnp.concatenate([d1, d2, d1, d2, d3, d1], axis=0)
            left = jnp.concatenate([d1, d1, d2, d2, d1, d3], axis=0)[:, 0:128]
            change = mm(left, right, TN)
            w_ref[m, r0 + b : 128, :] -= change[r0 + b : 128]


def kernel(
    x_ref, c_ref, skel_ref, near_ref, codes_ref, pick_ref,
    pot_ref, transfer_ref,
    sf, qf, sg, lists, list_sm, sib_s, sib_pick, left, right, basis, near_sum,
    norms, tiles, h_out, h_far, h_in, h_own, w, t_send, t_recv,
    s_send, s_recv, q_send, q_recv, n_send, n_recv, x_send, x_recv, f_send, f_recv,
    h_send, h_recv, l_send, l_recv, b_send, b_recv, local_sem,
):
    wide, sib = lax.axis_index("wide"), lax.axis_index("sib")
    x, z = wide // ZN, wide % ZN
    odd = sib % 2
    above, below = (x * ZN + (z + 1) % ZN, sib), (x * ZN + (z + ZN - 1) % ZN, sib)
    peers = [None] + [((x + d) % XN * ZN + z, sib) for d in range(1, XN)]
    twin = (wide, sib + 1 - 2 * odd)

    barrier = pltpu.get_barrier_semaphore()
    for other in (above, below, *peers[1:], twin):
        pl.semaphore_signal(barrier, inc=1, device_id=other, device_id_type=MESH)

    def remote(src, dst, send, recv, device):
        return pltpu.make_async_remote_copy(
            src_ref=src, dst_ref=dst, send_sem=send, recv_sem=recv,
            device_id=device, device_id_type=MESH,
        )

    def ring(buf, send, recv):
        pairs = []
        for i in range(CHUNKS):
            pair = []
            for way, (plan, device, step) in enumerate(((UP, above, ZN - 1), (DOWN, below, 1))):
                slot, half = plan[i]
                rows = pl.ds(half * HALF, HALF)
                pair.append(
                    remote(
                        buf.at[slot, rows], buf.at[(slot + step) % ZN, rows],
                        send.at[way, i], recv.at[way, i], device,
                    )
                )
            pairs.append(pair)
        return pairs

    s_ring = ring(sf, s_send, s_recv)
    q_ring = [ring(qf[p], q_send.at[p], q_recv.at[p]) for p in range(PARTS)]
    n_ring = []
    for hop in range(4):
        up, down = (ZN - hop) % ZN, hop
        pair = [
            remote(norms.at[up], norms.at[up - 1 if hop else ZN - 1],
                   n_send.at[0, hop], n_recv.at[0, hop], above)
        ]
        if hop < 3:
            pair.append(
                remote(norms.at[down], norms.at[down + 1],
                       n_send.at[1, hop], n_recv.at[1, hop], below)
            )
        n_ring.append(pair)
    x_copies = [
        remote(sf.at[0], sg.at[XN - d], x_send.at[d], x_recv.at[XN - d], peers[d])
        for d in range(1, XN)
    ]
    x_arrivals = [
        remote(sf.at[0], sg.at[d], x_send.at[d], x_recv.at[d], peers[d]) for d in range(1, XN)
    ]
    l_copies = [
        remote(codes_ref, lists.at[XN - d], l_send.at[d], l_recv.at[XN - d], peers[d])
        for d in range(1, XN)
    ]
    l_arrivals = [
        remote(codes_ref, lists.at[d], l_send.at[d], l_recv.at[d], peers[d]) for d in range(1, XN)
    ]
    f_copies = [
        [
            remote(h_out[p].at[2, pl.ds(way * HALF, HALF)], h_far[p].at[way],
                   f_send.at[p, way], f_recv.at[p, way], peers[1 + 2 * way])
            for way in (0, 1)
        ]
        for p in range(PARTS)
    ]
    h_copies = [
        [
            remote(h_out[p].at[1 + 2 * way, pl.ds(half * HALF, HALF)],
                   h_in[p].at[way, pl.ds(half * HALF, HALF)],
                   h_send.at[p, way, half], h_recv.at[p, way, half], peers[1 + 2 * way])
            for way in (0, 1)
            for half in (0, 1)
        ]
        for p in range(PARTS)
    ]
    mine, theirs = odd * HALF, HALF - odd * HALF
    pick_copy = remote(pick_ref, sib_pick, b_send.at[0], b_recv.at[0], twin)
    sib_copy = remote(sf.at[0, pl.ds(theirs, HALF)], sib_s, b_send.at[1], b_recv.at[1], twin)
    t_copy = remote(t_send, t_recv, b_send.at[2], b_recv.at[2], twin)

    def start(copies, *chunks):
        for i in chunks:
            for way in (0, 1):
                if i >= 2:
                    copies[i - 2][way].wait_recv()
                copies[i][way].start()

    def start_norms(hop):
        for way, copy in enumerate(n_ring[hop]):
            if hop:
                n_ring[hop - 1][way].wait_recv()
            copy.start()

    def skeleton(g):
        sf[0, g] = pick_rows(skel_ref[pl.ds(g, 1), :], x_ref[g])

    @pl.loop(0, HALF // 2)
    def _(i):
        skeleton(2 * i)
        skeleton(2 * i + 1)

    pl.semaphore_wait(barrier, 6)
    s_ring[0][0].start()
    s_ring[1][1].start()
    pick_copy.start()
    for copy in l_copies:
        copy.start()

    @pl.loop(HALF // 2, HALF)
    def _(i):
        skeleton(2 * i)
        skeleton(2 * i + 1)

    s_ring[0][1].start()
    s_ring[1][0].start()
    sib_copy.start()
    for copy in x_copies:
        copy.start()

    def compress(g):
        pts, skel_pts = x_ref[g], sf[0, g]
        row = half_rows(skel_pts)[0:1]
        norms[0, pl.ds(g, 1), :] = row
        block = kernel_exp(mm(pts, skel_pts, NT), half_col(pts), row).astype(BF16)
        basis[g] = block
        squeezed = mm(c_ref[g], block, TN).astype(BF16)
        for p in range(PARTS):
            qf[p][0, g] = squeezed[STARTS[p] : STARTS[p] + COLS[p]]

    @pl.loop(0, LEAVES // 2, unroll=2)
    def _(i):
        compress(2 * i)
        compress(2 * i + 1)

    start(q_ring[0], 0, 1)
    start_norms(0)

    @pl.loop(0, LEAVES, unroll=4)
    def _(g):
        near_prepare(x_ref, left, right, g)

    def near(first, last):
        @pl.loop(first, last, unroll=2)
        def _(g):
            near_sum[g] = near_leaf(left, right, c_ref, near_ref, g)

    near(0, 6)
    start(s_ring, 2)
    near(6, 8)
    start(s_ring, 3)
    near(8, 12)
    start(q_ring[0], 2)
    near(12, 14)
    start(q_ring[0], 3)
    start_norms(1)
    near(14, 16)
    start(s_ring, 4)
    start(q_ring[1], 0, 1)

    pick_copy.wait_recv()
    sib_copy.wait_recv()

    @pl.loop(0, HALF // 2)
    def _(i):
        for m in (2 * i, 2 * i + 1):
            own, other = sf[0, mine + m], sib_s[m]
            own_pick = pick_ref[pl.ds(mine + m, 1), :]
            other_pick = sib_pick[pl.ds(mine + m, 1), :]
            build_parent(
                w, m,
                jnp.where(odd == 1, other, own), jnp.where(odd == 1, own, other),
                jnp.where(odd == 1, other_pick, own_pick),
                jnp.where(odd == 1, own_pick, other_pick),
            )

    start(s_ring, 5)
    start_norms(2)
    factor_panel(w, 0)
    start(q_ring[0], 4)
    start(s_ring, 6)
    start_norms(3)
    factor_panel(w, 1)
    start(q_ring[0], 5)
    start(q_ring[1], 2)
    factor_panel(w, 2)
    start(q_ring[0], 6)
    start(q_ring[1], 3)
    factor_panel(w, 3)

    @pl.loop(0, HALF)
    def _(m):
        ta = w[m, :, 128:256].T * 16.0
        tb = w[m, :, 256:384].T * 16.0
        transfer_ref[mine + m] = jnp.where(odd == 1, tb, ta)
        t_send[m] = jnp.where(odd == 1, ta, tb)

    t_copy.start()

    for copy in l_arrivals:
        copy.wait_recv()
    list_copies = [
        pltpu.make_async_copy(codes_ref if d == 0 else lists.at[d], list_sm.at[d], local_sem.at[d])
        for d in range(XN)
    ]
    for copy in list_copies:
        copy.start()
    for copy in (*s_ring[5], *s_ring[6], *x_arrivals, n_ring[2][1], n_ring[3][0]):
        copy.wait_recv()
    for copy in list_copies:
        copy.wait()

    def entry(d, g, k):
        code = list_sm[d, 0, g * 4 + k]
        ahead = 1 + (code >> 4)
        there = ((z + ahead >> 3) + d & XN - 1) == 0
        return there, ahead & ZN - 1, code & LEAVES - 1

    def couple(d):
        @pl.loop(0, LEAVES, unroll=4)
        def _(g):
            pts = sf[0, g] if d == 0 else sg[d, g]
            col = half_col(pts)
            rows, named = [], []
            for k in range(4):
                there, slot, leaf = entry(d, g, k)
                rows.append(norms[slot, pl.ds(leaf, 1), :] + jnp.where(there, 0.0, -1e30))
                named.append(sf[slot, leaf])
            inner = mm(pts, jnp.concatenate(named, axis=0), NT)
            col = jnp.concatenate([col] * 4, axis=1)
            tiles[d, g] = kernel_exp(inner, col, jnp.concatenate(rows, axis=1)).astype(BF16)

    couple(2)
    start(q_ring[1], 4)
    couple(1)
    start(q_ring[1], 5)
    couple(3)
    couple(0)

    def partial(p, d, first, last, out):
        @pl.loop(first, last, unroll=8)
        def _(g):
            named = []
            for k in range(4):
                _, slot, leaf = entry(d, g, k)
                named.append(qf[p][slot, leaf])
            out(g, mm(jnp.concatenate(named, axis=1), tiles[d, g], NT))

    def far_part(p):
        for way in (0, 1):
            for i in (5, 6):
                q_ring[p][i][way].wait_recv()

        def put_far(g, total):
            h_out[p][2, g] = total.astype(BF16)

        def put_own(g, total):
            h_own[p][g] = total

        partial(p, 2, 0, LEAVES, put_far)
        for way in (0, 1):
            f_copies[p][way].start()
        if p == 0:
            start(q_ring[1], 6)
        for way in (0, 1):
            d = 1 + 2 * way

            def put(g, total, d=d):
                h_out[p][d, g] = total.astype(BF16)

            partial(p, d, HALF - way * HALF, LEAVES - way * HALF, put)
            h_copies[p][way * 2 + 1 - way].start()
        partial(p, 0, 0, LEAVES, put_own)
        for way in (0, 1):
            d = 1 + 2 * way

            def put_sum(g, total, d=d, way=way):
                total = total + h_far[p][way, g - way * HALF].astype(F32)
                h_out[p][d, g] = total.astype(BF16)

            f_copies[p][way].wait_recv()
            partial(p, d, way * HALF, HALF + way * HALF, put_sum)
            h_copies[p][way * 2 + way].start()

    far_part(0)

    t_copy.wait_recv()

    @pl.loop(0, HALF)
    def _(m):
        transfer_ref[theirs + m] = t_recv[m]

    far_part(1)
    for copies in h_copies:
        for copy in copies:
            copy.wait_recv()

    @pl.loop(0, LEAVES // 2)
    def _(i):
        for g in (2 * i, 2 * i + 1):
            total = []
            for p in range(PARTS):
                share = h_own[p][g] + h_in[p][0, g].astype(F32) + h_in[p][1, g].astype(F32)
                total.append(share.astype(BF16))
            value = near_sum[g] + mm(basis[g], jnp.concatenate(total, axis=0), NT)
            pot_ref[g] = value.astype(BF16)

    sent = [*s_ring, *n_ring, x_copies, l_copies, *f_copies, *h_copies]
    for p in range(PARTS):
        sent.extend(q_ring[p])
    for copies in (*sent, (pick_copy, sib_copy, t_copy)):
        for copy in copies:
            copy.wait_send()


def body(points, charges, skel, near_list, far_gap, far_leaf, par_pick):
    x = points.reshape(LEAVES, 256, 128)
    c = charges.reshape(LEAVES, 256, 128)
    codes = (far_gap * LEAVES + far_leaf).reshape(1, 64)
    codes = jnp.pad(codes, ((0, 7), (0, 64)))
    vmem = pl.BlockSpec(memory_space=pltpu.VMEM)
    smem = pl.BlockSpec(memory_space=pltpu.SMEM)
    block = (LEAVES, 128, 128)
    pot, transfer = pl.pallas_call(
        kernel,
        out_shape=(
            jax.ShapeDtypeStruct((LEAVES, 256, 128), BF16),
            jax.ShapeDtypeStruct((LEAVES, 128, 128), F32),
        ),
        in_specs=[vmem, vmem, vmem, smem, vmem, vmem],
        out_specs=(vmem, vmem),
        scratch_shapes=[
            pltpu.VMEM((ZN, *block), BF16),
            [pltpu.VMEM((ZN, LEAVES, n, 128), BF16) for n in COLS],
            pltpu.VMEM((XN, *block), BF16),
            pltpu.VMEM((XN, 8, 128), jnp.int32),
            pltpu.SMEM((XN, 8, 128), jnp.int32),
            pltpu.VMEM((HALF, 128, 128), BF16),
            pltpu.VMEM((LEAVES, 64), jnp.int32),
            pltpu.VMEM((LEAVES, 256, 256), BF16),
            pltpu.VMEM((LEAVES, 256, 256), BF16),
            pltpu.VMEM((LEAVES, 256, 128), BF16),
            pltpu.VMEM((LEAVES, 256, 128), F32),
            pltpu.VMEM((ZN, LEAVES, 128), F32),
            pltpu.VMEM((XN, LEAVES, 128, 512), BF16),
            [pltpu.VMEM((XN, LEAVES, n, 128), BF16) for n in COLS],
            [pltpu.VMEM((2, HALF, n, 128), BF16) for n in COLS],
            [pltpu.VMEM((2, LEAVES, n, 128), BF16) for n in COLS],
            [pltpu.VMEM((LEAVES, n, 128), F32) for n in COLS],
            pltpu.VMEM((HALF, 128, 384), F32),
            pltpu.VMEM((HALF, 128, 128), F32),
            pltpu.VMEM((HALF, 128, 128), F32),
            pltpu.SemaphoreType.DMA((2, CHUNKS)),
            pltpu.SemaphoreType.DMA((2, CHUNKS)),
            pltpu.SemaphoreType.DMA((PARTS, 2, CHUNKS)),
            pltpu.SemaphoreType.DMA((PARTS, 2, CHUNKS)),
            pltpu.SemaphoreType.DMA((2, 4)),
            pltpu.SemaphoreType.DMA((2, 4)),
            pltpu.SemaphoreType.DMA((XN,)),
            pltpu.SemaphoreType.DMA((XN,)),
            pltpu.SemaphoreType.DMA((PARTS, 2)),
            pltpu.SemaphoreType.DMA((PARTS, 2)),
            pltpu.SemaphoreType.DMA((PARTS, 2, 2)),
            pltpu.SemaphoreType.DMA((PARTS, 2, 2)),
            pltpu.SemaphoreType.DMA((XN,)),
            pltpu.SemaphoreType.DMA((XN,)),
            pltpu.SemaphoreType.DMA((3,)),
            pltpu.SemaphoreType.DMA((3,)),
            pltpu.SemaphoreType.DMA((XN,)),
        ],
        compiler_params=pltpu.CompilerParams(
            collective_id=0, has_side_effects=True, vmem_limit_bytes=56 << 20
        ),
        cost_estimate=pl.CostEstimate(flops=5_000_000_000, bytes_accessed=5_000_000, transcendentals=10_000_000),
    )(x, c, skel, near_list, codes, par_pick)
    return pot.reshape(LEAVES * 256, 128), transfer


def solution(mesh):
    placed = P(("wide", "sib"), None)
    return jax.shard_map(
        body,
        mesh=mesh,
        in_specs=(placed,) * 7,
        out_specs=(placed, P(("wide", "sib"), None, None)),
        check_vma=False,
    )
```

```python
import functools
import math

import jax
import jax.numpy as jnp
from jax import lax
from jax.experimental import pallas as pl
from jax.experimental.pallas import tpu as pltpu
from jax.sharding import PartitionSpec as P

F32, BF16 = jnp.float32, jnp.bfloat16
RATE = 2.0 * 1.5 / 128 / math.log(2.0)
NN = (((1,), (0,)), ((), ()))
NT = (((1,), (1,)), ((), ()))
TN = (((0,), (0,)), ((), ()))
MESH = pl.DeviceIdType.MESH

LEAVES, HALF = 16, 8
XN, ZN = 4, 8
PANEL = 32
CHUNKS = 7
PARTS, STARTS, COLS = 2, (0, 64), (64, 64)
UP = [(0, 0), (0, 1), (7, 0), (7, 1), (6, 0), (6, 1), (5, 0)]
DOWN = [(0, 1), (0, 0), (1, 1), (1, 0), (2, 1), (2, 0), (3, 1)]


def mm(a, b, dims=NN):
    return lax.dot_general(a, b, dims, preferred_element_type=F32)


def squares(pts):
    wide = pts.astype(F32)
    sq = wide * wide
    high = sq.astype(BF16)
    return high, (sq - high.astype(F32)).astype(BF16)


def half_col(pts):
    high, low = squares(pts)
    ones = jnp.ones((128, 128), BF16)
    return -0.5 * (mm(high, ones) + mm(low, ones))


def half_rows(pts):
    high, low = squares(pts)
    ones = jnp.ones((16, 128), BF16)
    return (-0.5 * (mm(ones, high, NT) + mm(ones, low, NT)))[0:8]


def kernel_exp(inner, col, row):
    return jnp.exp2(RATE * (inner + (col + row)))


def three(x):
    a = x.astype(BF16)
    rest = x - a.astype(F32)
    b = rest.astype(BF16)
    return a, b, (rest - b.astype(F32)).astype(BF16)


def pick_rows(index_row, pts):
    place = lax.broadcasted_iota(jnp.int32, (pts.shape[0], index_row.shape[1]), 0)
    hot = jnp.where(place == index_row, 1.0, 0.0).astype(BF16)
    return mm(hot, pts, TN).astype(BF16)


def near_prepare(x_ref, left_ref, right_ref, g):
    pts = x_ref[g]
    n1, n2, n3 = three(half_col(pts))
    lane = lax.broadcasted_iota(jnp.int32, pts.shape, 1)
    one, zero = jnp.ones(pts.shape, BF16), jnp.zeros(pts.shape, BF16)

    def parts(at):
        rest = jnp.where(lane == at + 2, n3, zero)
        return jnp.where(lane == at, n1, jnp.where(lane == at + 1, n2, rest))

    left_ref[g, :, 0:128] = pts
    right_ref[g, :, 0:128] = pts
    left_ref[g, :, 128:256] = jnp.where((lane >= 3) & (lane < 6), one, parts(0))
    right_ref[g, :, 128:256] = jnp.where(lane < 3, one, parts(3))


def near_leaf(left_ref, right_ref, c_ref, near_ref, g):
    left = left_ref[g]
    total = None
    for k in range(near_ref.shape[1]):
        m = near_ref[g, k]
        tile = jnp.exp2(RATE * mm(left, right_ref[m], NT)).astype(BF16)
        term = mm(tile, c_ref[m])
        total = term if total is None else total + term
    return total


def build_parent(w_ref, m, sa, sb, pa, pb):
    par = jnp.concatenate([pick_rows(pa, sa), pick_rows(pb, sb)], axis=0)
    col = half_col(par)
    ea = kernel_exp(mm(par, sa, NT), col, half_rows(sa)[0:1])
    eb = kernel_exp(mm(par, sb, NT), col, half_rows(sb)[0:1])
    both = jnp.concatenate([ea, eb], axis=1)
    gram = lax.dot_general(
        both, both, NT, precision=lax.Precision.HIGHEST, preferred_element_type=F32
    )
    row = lax.broadcasted_iota(jnp.int32, (128, 128), 0)
    lane = lax.broadcasted_iota(jnp.int32, (128, 128), 1)
    w_ref[m, :, 0:128] = gram + jnp.where(row == lane, 1.0, 0.0)
    w_ref[m, :, 128:384] = both


def factor_panel(w_ref, p):
    r0, b, n = p * PANEL, PANEL, w_ref.shape[0]
    lane = lax.broadcasted_iota(jnp.int32, (1, b, 128), 2)
    row = lax.broadcasted_iota(jnp.int32, (1, b, 128), 1)
    slab = w_ref[:, r0 : r0 + b, 0:128]
    if r0:
        slab = pltpu.roll(slab, 128 - r0, 2)
    a = jnp.where(lane < b, slab, jnp.where(lane == row + b, 1.0, 0.0))
    diag = jnp.zeros((n, b, 128), F32)
    for j in range(b):
        col = jnp.broadcast_to(a[:, :, j : j + 1], (n, b, 128))
        piv = col[:, j : j + 1, :]
        top = a[:, j : j + 1, :] / piv
        diag = jnp.where(row == j, piv, diag)
        a = a - jnp.where(row > j, col, 0.0) * top
    root = lax.rsqrt(diag)
    root = root * (1.5 - 0.5 * diag * root * root)
    inv = pltpu.roll(jnp.where(lane < 2 * b, a, 0.0) * root, 128 - b, 2)
    for m in range(n):
        l1, l2, l3 = three(inv[m][:, 0:b])
        left = jnp.concatenate([l1, l1, l2, l2, l1, l3], axis=1)
        r1, r2, r3 = three(w_ref[m, r0 : r0 + b, :])
        right = jnp.concatenate([r1, r2, r1, r2, r3, r1], axis=0)
        done = mm(left, right)
        w_ref[m, r0 : r0 + b, :] = done
        if r0 + b < 128:
            d1, d2, d3 = three(done)
            right = jnp.concatenate([d1, d2, d1, d2, d3, d1], axis=0)
            left = jnp.concatenate([d1, d1, d2, d2, d1, d3], axis=0)[:, 0:128]
            change = mm(left, right, TN)
            w_ref[m, r0 + b : 128, :] -= change[r0 + b : 128]


def kernel(
    x_ref, c_ref, skel_ref, near_ref, gap_ref, leaf_ref, pick_ref,
    pot_ref, transfer_ref,
    sf, qf, sg, codes_ref, lists, list_sm, sib_s, sib_pick, left, right, basis, near_sum,
    norms, tiles, h_out, h_far, h_in, h_own, w, t_send, t_recv,
    s_send, s_recv, q_send, q_recv, n_send, n_recv, x_send, x_recv, f_send, f_recv,
    h_send, h_recv, l_send, l_recv, b_send, b_recv, local_sem,
):
    wide, sib = lax.axis_index("wide"), lax.axis_index("sib")
    x, z = wide // ZN, wide % ZN
    odd = sib % 2
    above, below = (x * ZN + (z + 1) % ZN, sib), (x * ZN + (z + ZN - 1) % ZN, sib)
    peers = [None] + [((x + d) % XN * ZN + z, sib) for d in range(1, XN)]
    twin = (wide, sib + 1 - 2 * odd)

    barrier = pltpu.get_barrier_semaphore()
    for other in (above, below, *peers[1:], twin):
        pl.semaphore_signal(barrier, inc=1, device_id=other, device_id_type=MESH)

    def remote(src, dst, send, recv, device):
        return pltpu.make_async_remote_copy(
            src_ref=src, dst_ref=dst, send_sem=send, recv_sem=recv,
            device_id=device, device_id_type=MESH,
        )

    def ring(buf, send, recv):
        pairs = []
        for i in range(CHUNKS):
            pair = []
            for way, (plan, device, step) in enumerate(((UP, above, ZN - 1), (DOWN, below, 1))):
                slot, half = plan[i]
                rows = pl.ds(half * HALF, HALF)
                pair.append(
                    remote(
                        buf.at[slot, rows], buf.at[(slot + step) % ZN, rows],
                        send.at[way, i], recv.at[way, i], device,
                    )
                )
            pairs.append(pair)
        return pairs

    s_ring = ring(sf, s_send, s_recv)
    q_ring = [ring(qf[p], q_send.at[p], q_recv.at[p]) for p in range(PARTS)]
    n_ring = []
    for hop in range(4):
        up, down = (ZN - hop) % ZN, hop
        pair = [
            remote(norms.at[up], norms.at[up - 1 if hop else ZN - 1],
                   n_send.at[0, hop], n_recv.at[0, hop], above)
        ]
        if hop < 3:
            pair.append(
                remote(norms.at[down], norms.at[down + 1],
                       n_send.at[1, hop], n_recv.at[1, hop], below)
            )
        n_ring.append(pair)
    x_copies = [
        remote(sf.at[0], sg.at[XN - d], x_send.at[d], x_recv.at[XN - d], peers[d])
        for d in range(1, XN)
    ]
    x_arrivals = [
        remote(sf.at[0], sg.at[d], x_send.at[d], x_recv.at[d], peers[d]) for d in range(1, XN)
    ]
    l_copies = [
        remote(codes_ref, lists.at[XN - d], l_send.at[d], l_recv.at[XN - d], peers[d])
        for d in range(1, XN)
    ]
    l_arrivals = [
        remote(codes_ref, lists.at[d], l_send.at[d], l_recv.at[d], peers[d]) for d in range(1, XN)
    ]
    f_copies = [
        [
            remote(h_out[p].at[2, pl.ds(way * HALF, HALF)], h_far[p].at[way],
                   f_send.at[p, way], f_recv.at[p, way], peers[1 + 2 * way])
            for way in (0, 1)
        ]
        for p in range(PARTS)
    ]
    h_copies = [
        [
            remote(h_out[p].at[1 + 2 * way, pl.ds(half * HALF, HALF)],
                   h_in[p].at[way, pl.ds(half * HALF, HALF)],
                   h_send.at[p, way, half], h_recv.at[p, way, half], peers[1 + 2 * way])
            for way in (0, 1)
            for half in (0, 1)
        ]
        for p in range(PARTS)
    ]
    mine, theirs = odd * HALF, HALF - odd * HALF
    pick_copy = remote(pick_ref, sib_pick, b_send.at[0], b_recv.at[0], twin)
    sib_copy = remote(sf.at[0, pl.ds(theirs, HALF)], sib_s, b_send.at[1], b_recv.at[1], twin)
    t_copy = remote(t_send, t_recv, b_send.at[2], b_recv.at[2], twin)

    def start(copies, *chunks):
        for i in chunks:
            for way in (0, 1):
                if i >= 2:
                    copies[i - 2][way].wait_recv()
                copies[i][way].start()

    def start_norms(hop):
        for way, copy in enumerate(n_ring[hop]):
            if hop:
                n_ring[hop - 1][way].wait_recv()
            copy.start()

    def skeleton(g):
        sf[0, g] = pick_rows(skel_ref[pl.ds(g, 1), :], x_ref[g])

    @pl.loop(0, HALF // 2)
    def _(i):
        skeleton(2 * i)
        skeleton(2 * i + 1)

    codes_ref[...] = jnp.zeros_like(codes_ref)
    codes_ref[:, 0:4] = gap_ref[...] * LEAVES + leaf_ref[...]
    pl.semaphore_wait(barrier, 6)
    s_ring[0][0].start()
    s_ring[1][1].start()
    pick_copy.start()
    for copy in l_copies:
        copy.start()

    @pl.loop(HALF // 2, HALF)
    def _(i):
        skeleton(2 * i)
        skeleton(2 * i + 1)

    s_ring[0][1].start()
    s_ring[1][0].start()
    sib_copy.start()
    for copy in x_copies:
        copy.start()

    def compress(g):
        pts, skel_pts = x_ref[g], sf[0, g]
        row = half_rows(skel_pts)[0:1]
        norms[0, pl.ds(g, 1), :] = row
        block = kernel_exp(mm(pts, skel_pts, NT), half_col(pts), row).astype(BF16)
        basis[g] = block
        squeezed = mm(c_ref[g], block, TN).astype(BF16)
        for p in range(PARTS):
            qf[p][0, g] = squeezed[STARTS[p] : STARTS[p] + COLS[p]]

    @pl.loop(0, LEAVES // 2, unroll=2)
    def _(i):
        compress(2 * i)
        compress(2 * i + 1)

    start(q_ring[0], 0, 1)
    start_norms(0)

    @pl.loop(0, LEAVES, unroll=4)
    def _(g):
        near_prepare(x_ref, left, right, g)

    def near(first, last):
        @pl.loop(first, last, unroll=2)
        def _(g):
            near_sum[g] = near_leaf(left, right, c_ref, near_ref, g)

    near(0, 6)
    start(s_ring, 2)
    near(6, 8)
    start(s_ring, 3)
    near(8, 12)
    start(q_ring[0], 2)
    near(12, 14)
    start(q_ring[0], 3)
    start_norms(1)
    near(14, 16)
    start(s_ring, 4)
    start(q_ring[1], 0, 1)

    pick_copy.wait_recv()
    sib_copy.wait_recv()

    @pl.loop(0, HALF // 2)
    def _(i):
        for m in (2 * i, 2 * i + 1):
            own, other = sf[0, mine + m], sib_s[m]
            own_pick = pick_ref[pl.ds(mine + m, 1), :]
            other_pick = sib_pick[pl.ds(mine + m, 1), :]
            build_parent(
                w, m,
                jnp.where(odd == 1, other, own), jnp.where(odd == 1, own, other),
                jnp.where(odd == 1, other_pick, own_pick),
                jnp.where(odd == 1, own_pick, other_pick),
            )

    start(s_ring, 5)
    start_norms(2)
    factor_panel(w, 0)
    start(q_ring[0], 4)
    start(s_ring, 6)
    start_norms(3)
    factor_panel(w, 1)
    start(q_ring[0], 5)
    start(q_ring[1], 2)
    factor_panel(w, 2)
    start(q_ring[0], 6)
    start(q_ring[1], 3)
    factor_panel(w, 3)

    @pl.loop(0, HALF)
    def _(m):
        ta = w[m, :, 128:256].T * 16.0
        tb = w[m, :, 256:384].T * 16.0
        transfer_ref[mine + m] = jnp.where(odd == 1, tb, ta)
        t_send[m] = jnp.where(odd == 1, ta, tb)

    t_copy.start()

    for copy in l_arrivals:
        copy.wait_recv()
    list_copies = [
        pltpu.make_async_copy(codes_ref if d == 0 else lists.at[d], list_sm.at[d], local_sem.at[d])
        for d in range(XN)
    ]
    for copy in list_copies:
        copy.start()
    for copy in (*s_ring[5], *s_ring[6], *x_arrivals, n_ring[2][1], n_ring[3][0]):
        copy.wait_recv()
    for copy in list_copies:
        copy.wait()

    def entry(d, g, k):
        code = list_sm[d, g, k]
        ahead = 1 + (code >> 4)
        there = ((z + ahead >> 3) + d & XN - 1) == 0
        return there, ahead & ZN - 1, code & LEAVES - 1

    def couple(d):
        @pl.loop(0, LEAVES, unroll=4)
        def _(g):
            pts = sf[0, g] if d == 0 else sg[d, g]
            col = half_col(pts)
            rows, named = [], []
            for k in range(4):
                there, slot, leaf = entry(d, g, k)
                rows.append(norms[slot, pl.ds(leaf, 1), :] + jnp.where(there, 0.0, -1e30))
                named.append(sf[slot, leaf])
            inner = mm(pts, jnp.concatenate(named, axis=0), NT)
            col = jnp.concatenate([col] * 4, axis=1)
            tiles[d, g] = kernel_exp(inner, col, jnp.concatenate(rows, axis=1)).astype(BF16)

    couple(2)
    start(q_ring[1], 4)
    couple(1)
    start(q_ring[1], 5)
    couple(3)
    couple(0)

    def partial(p, d, first, last, out):
        @pl.loop(first, last, unroll=8)
        def _(g):
            named = []
            for k in range(4):
                _, slot, leaf = entry(d, g, k)
                named.append(qf[p][slot, leaf])
            out(g, mm(jnp.concatenate(named, axis=1), tiles[d, g], NT))

    def far_part(p):
        for way in (0, 1):
            for i in (5, 6):
                q_ring[p][i][way].wait_recv()

        def put_far(g, total):
            h_out[p][2, g] = total.astype(BF16)

        def put_own(g, total):
            h_own[p][g] = total

        partial(p, 2, 0, LEAVES, put_far)
        for way in (0, 1):
            f_copies[p][way].start()
        if p == 0:
            start(q_ring[1], 6)
        for way in (0, 1):
            d = 1 + 2 * way

            def put(g, total, d=d):
                h_out[p][d, g] = total.astype(BF16)

            partial(p, d, HALF - way * HALF, LEAVES - way * HALF, put)
            h_copies[p][way * 2 + 1 - way].start()
        partial(p, 0, 0, LEAVES, put_own)
        for way in (0, 1):
            d = 1 + 2 * way

            def put_sum(g, total, d=d, way=way):
                total = total + h_far[p][way, g - way * HALF].astype(F32)
                h_out[p][d, g] = total.astype(BF16)

            f_copies[p][way].wait_recv()
            partial(p, d, way * HALF, HALF + way * HALF, put_sum)
            h_copies[p][way * 2 + way].start()

    far_part(0)

    t_copy.wait_recv()

    @pl.loop(0, HALF)
    def _(m):
        transfer_ref[theirs + m] = t_recv[m]

    far_part(1)
    for copies in h_copies:
        for copy in copies:
            copy.wait_recv()

    @pl.loop(0, LEAVES // 2)
    def _(i):
        for g in (2 * i, 2 * i + 1):
            total = []
            for p in range(PARTS):
                share = h_own[p][g] + h_in[p][0, g].astype(F32) + h_in[p][1, g].astype(F32)
                total.append(share.astype(BF16))
            value = near_sum[g] + mm(basis[g], jnp.concatenate(total, axis=0), NT)
            pot_ref[g] = value.astype(BF16)

    sent = [*s_ring, *n_ring, x_copies, l_copies, *f_copies, *h_copies]
    for p in range(PARTS):
        sent.extend(q_ring[p])
    for copies in (*sent, (pick_copy, sib_copy, t_copy)):
        for copy in copies:
            copy.wait_send()


def body(points, charges, skel, near_list, far_gap, far_leaf, par_pick):
    x = points.reshape(LEAVES, 256, 128)
    c = charges.reshape(LEAVES, 256, 128)
    vmem = pl.BlockSpec(memory_space=pltpu.VMEM)
    smem = pl.BlockSpec(memory_space=pltpu.SMEM)
    block = (LEAVES, 128, 128)
    pot, transfer = pl.pallas_call(
        kernel,
        out_shape=(
            jax.ShapeDtypeStruct((LEAVES, 256, 128), BF16),
            jax.ShapeDtypeStruct((LEAVES, 128, 128), F32),
        ),
        in_specs=[vmem, vmem, vmem, smem, vmem, vmem, vmem],
        out_specs=(vmem, vmem),
        scratch_shapes=[
            pltpu.VMEM((ZN, *block), BF16),
            [pltpu.VMEM((ZN, LEAVES, n, 128), BF16) for n in COLS],
            pltpu.VMEM((XN, *block), BF16),
            pltpu.VMEM((LEAVES, 128), jnp.int32),
            pltpu.VMEM((XN, LEAVES, 128), jnp.int32),
            pltpu.SMEM((XN, LEAVES, 128), jnp.int32),
            pltpu.VMEM((HALF, 128, 128), BF16),
            pltpu.VMEM((LEAVES, 64), jnp.int32),
            pltpu.VMEM((LEAVES, 256, 256), BF16),
            pltpu.VMEM((LEAVES, 256, 256), BF16),
            pltpu.VMEM((LEAVES, 256, 128), BF16),
            pltpu.VMEM((LEAVES, 256, 128), F32),
            pltpu.VMEM((ZN, LEAVES, 128), F32),
            pltpu.VMEM((XN, LEAVES, 128, 512), BF16),
            [pltpu.VMEM((XN, LEAVES, n, 128), BF16) for n in COLS],
            [pltpu.VMEM((2, HALF, n, 128), BF16) for n in COLS],
            [pltpu.VMEM((2, LEAVES, n, 128), BF16) for n in COLS],
            [pltpu.VMEM((LEAVES, n, 128), F32) for n in COLS],
            pltpu.VMEM((HALF, 128, 384), F32),
            pltpu.VMEM((HALF, 128, 128), F32),
            pltpu.VMEM((HALF, 128, 128), F32),
            pltpu.SemaphoreType.DMA((2, CHUNKS)),
            pltpu.SemaphoreType.DMA((2, CHUNKS)),
            pltpu.SemaphoreType.DMA((PARTS, 2, CHUNKS)),
            pltpu.SemaphoreType.DMA((PARTS, 2, CHUNKS)),
            pltpu.SemaphoreType.DMA((2, 4)),
            pltpu.SemaphoreType.DMA((2, 4)),
            pltpu.SemaphoreType.DMA((XN,)),
            pltpu.SemaphoreType.DMA((XN,)),
            pltpu.SemaphoreType.DMA((PARTS, 2)),
            pltpu.SemaphoreType.DMA((PARTS, 2)),
            pltpu.SemaphoreType.DMA((PARTS, 2, 2)),
            pltpu.SemaphoreType.DMA((PARTS, 2, 2)),
            pltpu.SemaphoreType.DMA((XN,)),
            pltpu.SemaphoreType.DMA((XN,)),
            pltpu.SemaphoreType.DMA((3,)),
            pltpu.SemaphoreType.DMA((3,)),
            pltpu.SemaphoreType.DMA((XN,)),
        ],
        compiler_params=pltpu.CompilerParams(
            collective_id=0, has_side_effects=True, vmem_limit_bytes=56 << 20
        ),
        cost_estimate=pl.CostEstimate(flops=5_000_000_000, bytes_accessed=5_000_000, transcendentals=10_000_000),
    )(x, c, skel, near_list, far_gap, far_leaf, par_pick)
    return pot.reshape(LEAVES * 256, 128), transfer


def solution(mesh):
    placed = P(("wide", "sib"), None)
    return jax.shard_map(
        body,
        mesh=mesh,
        in_specs=(placed,) * 7,
        out_specs=(placed, P(("wide", "sib"), None, None)),
        check_vma=False,
    )
```
